32 devices in a mesh: dp: 4 (over y, x), ctx: 8 (over z, core).
Axes of the slice: x: 2, y: 2, z: 4, core: 2. Of those that a mesh axis runs over, the one named last changes fastest.
Arguments:
- inputs: bfloat16 [1024, 8, 1088], P('ctx', 'dp'), may hold values from -6 to 6
- segments: int32 [8, 1024], P('dp', 'ctx'), may hold values from 0 to 3, as said below
- ln1_gain: float32 [1088], replicated, may hold values from 0.1 to 1.9
- ln1_bias: float32 [1088], replicated, may hold values from -3 to 3
- qkv_weight: bfloat16 [1088, 3264], P('ctx', 'dp'), may hold values from -0.1875 to 0.1875
- query_bias: float32 [1088], replicated, may hold values from -3 to 3
- value_bias: float32 [1088], replicated, may hold values from -3 to 3
- proj_weight: bfloat16 [1088, 1088], P('ctx', 'dp'), may hold values from -0.5 to 0.5
- proj_bias: float32 [1088], replicated, may hold values from -3 to 3
- ln2_gain: float32 [1088], replicated, may hold values from 0.1 to 1.9
- ln2_bias: float32 [1088], replicated, may hold values from -3 to 3
- fc_weight: bfloat16 [1088, 4352], P(None, ('dp', 'ctx')), may hold values from -0.1875 to 0.1875
- fc_bias: bfloat16 [4352], P(('dp', 'ctx')), may hold values from -3 to 3
- out_weight: bfloat16 [4352, 1088], P(('dp', 'ctx')), may hold values from -0.09375 to 0.09375
- out_bias: float32 [1088], replicated, may hold values from -3 to 3
- cotangent: bfloat16 [1024, 8, 1088], P('ctx', 'dp'), may hold values from -6 to 6
Outputs:
- output: bfloat16 [1024, 8, 1088], P('ctx', 'dp')
- input_grad: bfloat16 [1024, 8, 1088], P('ctx', 'dp')
- ln1_gain_grad: float32 [1088], replicated
- ln1_bias_grad: float32 [1088], replicated
- qkv_weight_grad: float32 [1088, 3264], P('ctx', 'dp')
- query_bias_grad: float32 [1088], replicated
- value_bias_grad: float32 [1088], replicated
- proj_weight_grad: float32 [1088, 1088], P('ctx', 'dp')
- proj_bias_grad: float32 [1088], replicated
- ln2_gain_grad: float32 [1088], replicated
- ln2_bias_grad: float32 [1088], replicated
- fc_weight_grad: float32 [1088, 4352], P(None, ('dp', 'ctx'))
- fc_bias_grad: float32 [4352], P(('dp', 'ctx'))
- out_weight_grad: float32 [4352, 1088], P(('dp', 'ctx'))
- out_bias_grad: float32 [1088], replicated
The draws below stay inside these ranges and needn't reach their ends.
Inputs may be any that keep to these rules, and one draw needn't show every extreme that they name: `segments`: segment numbers start at 0 in every sequence and never fall along it. In every aligned run of 2 sequences, one sequence is a single document.
All inputs are finite; a program needn't handle non-finite values.
Results may differ from the reference program's by a relative error of at most 0.02.
Values may be sent and summed in bfloat16 or wider, within the bound.
A program may use at most 320 MiB of HBM per device.

```python
import math
import jax
import jax.numpy as jnp
from jax import lax

D = 1088
HEADS = 17
HEAD_DIM = 64
FF = 4352
SEQ_MB = 1
MICRO = 2
BOUNDS = 3
LENGTH = 1024
NSEQ = 8


def draw_segments(key, part):
    key = jax.random.fold_in(key, 7)
    cut_key, pick_key = jax.random.split(key)
    cut_points = jax.random.randint(cut_key, (NSEQ, BOUNDS), 1, LENGTH)
    group_seqs = MICRO * SEQ_MB
    chosen = jax.random.randint(pick_key, (NSEQ // group_seqs,), 0, group_seqs)
    seq_index = jnp.arange(NSEQ, dtype=jnp.int32)
    single = seq_index % group_seqs == chosen[seq_index // group_seqs]
    cut_points = jnp.where(single[:, None], LENGTH, cut_points)
    positions = jnp.arange(LENGTH, dtype=jnp.int32)
    passed = (positions[None, :, None] >= cut_points[:, None, :]).astype(jnp.int32)
    return jnp.sum(passed, -1).astype(jnp.int32)


def block_levels(rng, shape, cuts, smallest, largest):
    gain, own = 1.0, jax.random.fold_in(rng, 6)
    for dim, blocks in cuts:
        draws = jnp.exp(jax.random.uniform(jax.random.fold_in(own, dim), (blocks,), jnp.float32, smallest / len(cuts), largest / len(cuts)))
        gain = gain * jnp.repeat(draws, shape[dim] // blocks).reshape([-1 if axis == dim else 1 for axis in range(len(shape))])
    return gain


def normal_values(rng, dims, scale, bound, cuts=(), kind=jnp.bfloat16):
    factor_of = block_levels(rng, dims, cuts, -0.22, 0.18) if cuts else 1.0
    values = jax.random.normal(rng, dims, jnp.float32) * scale * factor_of
    return jnp.minimum(jnp.maximum(values, -bound), bound).astype(kind)


def setup_inputs(seed: int = 0) -> dict:
    key_of = jax.random.split(jax.random.key(seed), 17)
    inputs = normal_values(key_of[0], (LENGTH, NSEQ, D), 1.0, 6.0, ((0, 8), (1, 4)))
    segments = draw_segments(jax.random.fold_in(key_of[16], 71), 0)
    ln1_gain = jnp.clip(1.0 + 0.18 * jax.random.normal(key_of[2], (D,), jnp.float32), 0.1, 1.9)
    ln1_bias = normal_values(key_of[3], (D,), 0.3, 3.0, (), jnp.float32)
    qkv_weight = normal_values(key_of[4], (D, 3 * D), D ** -0.5, 0.1875, ((0, 8), (1, 4)))
    query_bias = normal_values(key_of[5], (D,), 0.3, 3.0, (), jnp.float32)
    value_bias = normal_values(key_of[6], (D,), 0.3, 3.0, (), jnp.float32)
    proj_weight = normal_values(key_of[7], (D, D), (D // 8) ** -0.5, 0.5, ((0, 8), (1, 4)))
    proj_bias = normal_values(key_of[8], (D,), 0.3, 3.0, (), jnp.float32)
    ln2_gain = jnp.clip(1.0 + 0.18 * jax.random.normal(key_of[9], (D,), jnp.float32), 0.1, 1.9)
    ln2_bias = normal_values(key_of[10], (D,), 0.3, 3.0, (), jnp.float32)
    fc_weight = normal_values(key_of[11], (D, FF), D ** -0.5, 0.1875, ((1, 32),))
    fc_bias = normal_values(key_of[12], (FF,), 0.3, 3.0, ((0, 32),))
    out_weight = normal_values(key_of[13], (FF, D), FF ** -0.5, 0.09375, ((0, 32),))
    out_bias = normal_values(key_of[14], (D,), 0.3, 3.0, (), jnp.float32)
    cotangent = normal_values(key_of[15], (LENGTH, NSEQ, D), 1.0, 6.0, ((0, 8), (1, 4)))
    return dict(inputs=inputs, segments=segments, ln1_gain=ln1_gain, ln1_bias=ln1_bias, qkv_weight=qkv_weight, query_bias=query_bias, value_bias=value_bias, proj_weight=proj_weight, proj_bias=proj_bias, ln2_gain=ln2_gain, ln2_bias=ln2_bias, fc_weight=fc_weight, fc_bias=fc_bias, out_weight=out_weight, out_bias=out_bias, cotangent=cotangent)


@jax.custom_vjp
def low(v):
    return lax.optimization_barrier(v.astype(jnp.bfloat16)).astype(jnp.float32)

@jax.custom_vjp
def low_back(v):
    return v

def low_keep(v):
    return (low(v), None)

def low_pass(kept, grad):
    return (grad,)

def back_keep(v):
    return (v, None)

def back_low(kept, grad):
    return (low(grad),)
low.defvjp(low_keep, low_pass)
low_back.defvjp(back_keep, back_low)
EPSILON = 1e-05
MASKED = -1e+30
HIGHEST = lax.Precision.HIGHEST

def normalize(values, gain_row, shift_row):
    center = values - lax.optimization_barrier(jnp.mean(values, -1, keepdims=True))
    spread = lax.optimization_barrier(jnp.mean(center * center, -1, keepdims=True))
    return center * lax.rsqrt(spread + EPSILON) * gain_row + shift_row

def matmul(operand, weight):
    return jnp.einsum('lgd,dn->lgn', operand, weight, precision=HIGHEST)

def forward(inputs, segments, ln1_gain, ln1_bias, qkv_weight, query_bias, value_bias, proj_weight, proj_bias, ln2_gain, ln2_bias, fc_weight, fc_bias, out_weight, out_bias):
    seq_length, group_seqs, model_width = inputs.shape
    normed = low(normalize(inputs, ln1_gain, ln1_bias))
    qkv_bias = jnp.concatenate([query_bias, jnp.zeros_like(query_bias), value_bias])
    joined = low_back(matmul(normed, qkv_weight) + qkv_bias)
    queries = low(joined[..., :model_width]).reshape(seq_length, group_seqs, HEADS, HEAD_DIM)
    key_rows = low(joined[..., model_width:2 * model_width]).reshape(seq_length, group_seqs, HEADS, HEAD_DIM)
    value_rows = low(joined[..., 2 * model_width:]).reshape(seq_length, group_seqs, HEADS, HEAD_DIM)
    block_rows = math.gcd(seq_length, 512)
    positions = jnp.arange(seq_length, dtype=jnp.int32)
    score_scale = HEAD_DIM ** (-0.5)

    def attend(first_row):
        query_block = lax.dynamic_slice_in_dim(queries, first_row, block_rows, 0)
        query_segments = lax.dynamic_slice_in_dim(segments, first_row, block_rows, 1)
        query_pos = first_row + jnp.arange(block_rows, dtype=jnp.int32)
        scores = low_back(jnp.einsum('qghe,kghe->ghqk', query_block, key_rows, precision=HIGHEST)) * score_scale
        causal = positions[None, :] <= query_pos[:, None]
        allowed = causal[None, None] & (query_segments[:, None, :, None] == segments[:, None, None, :])
        scores = jnp.where(allowed, scores, MASKED)
        row_max = lax.optimization_barrier(jnp.max(scores, -1, keepdims=True))
        powers = jnp.exp(scores - row_max)
        weights = low(powers / lax.optimization_barrier(jnp.sum(powers, -1, keepdims=True)))
        mixed = jnp.einsum('ghqk,kghe->qghe', weights, value_rows, precision=HIGHEST)
        return mixed.reshape(block_rows, group_seqs, model_width)
    starts = jnp.arange(0, seq_length, block_rows, dtype=jnp.int32)
    attended = lax.map(jax.checkpoint(attend), starts).reshape(seq_length, group_seqs, model_width)
    attended = low(low_back(attended))
    resid = inputs + low_back(matmul(attended, proj_weight) + proj_bias)
    hidden_in = low(normalize(resid, ln2_gain, ln2_bias))
    activated = low(jax.nn.gelu(low_back(matmul(hidden_in, fc_weight) + fc_bias), approximate=True))
    return resid + low_back(matmul(activated, out_weight) + out_bias)

def reference(inputs, segments, ln1_gain, ln1_bias, qkv_weight, query_bias, value_bias, proj_weight, proj_bias, ln2_gain, ln2_bias, fc_weight, fc_bias, out_weight, out_bias, cotangent):
    group_seqs = math.gcd(NSEQ, max(1, 4096 // LENGTH))
    groups_count = NSEQ // group_seqs
    params = tuple((element.astype(jnp.float32) for element in (ln1_gain, ln1_bias, qkv_weight, query_bias, value_bias, proj_weight, proj_bias, ln2_gain, ln2_bias, fc_weight, fc_bias, out_weight, out_bias)))
    inputs_split = jnp.moveaxis(inputs.astype(jnp.float32).reshape(LENGTH, groups_count, group_seqs, D), 1, 0)
    cotan_split = jnp.moveaxis(cotangent.astype(jnp.float32).reshape(LENGTH, groups_count, group_seqs, D), 1, 0)
    segment_split = segments.reshape(groups_count, group_seqs, LENGTH)

    def run_group(totals, element):
        group_inputs, cotan_rows, group_segments = element

        def apply_layer(values, *weights):
            return forward(values, group_segments, *weights)
        result, pullback = jax.vjp(apply_layer, group_inputs, *params)
        gradients = pullback(cotan_rows)
        totals = tuple((summed + addend for summed, addend in zip(totals, gradients[1:])))
        return (totals, (result, gradients[0]))
    zero_totals = tuple((jnp.zeros_like(element) for element in params))
    totals, (results, input_grads) = lax.scan(run_group, zero_totals, (inputs_split, cotan_split, segment_split))
    output = jnp.moveaxis(results, 0, 1).reshape(LENGTH, NSEQ, D).astype(jnp.bfloat16)
    input_grad = jnp.moveaxis(input_grads, 0, 1).reshape(LENGTH, NSEQ, D).astype(jnp.bfloat16)
    return (output, input_grad) + tuple(totals)
```

```python
import functools

import jax
import jax.numpy as jnp
from jax import lax
from jax.experimental import pallas as pl
from jax.experimental.pallas import tpu as pltpu
from jax.sharding import Mesh
from jax.sharding import PartitionSpec as P

HEADS = 17
HEAD_DIM = 64
EPSILON = 1e-05
MASKED = -1e30
SCALE = HEAD_DIM ** (-0.5)
GROUP = ("dp", "z")
EVERY = ("dp", "z", "core")
BF16 = jnp.bfloat16
F32 = jnp.float32
VMEM_BYTES = 48 * 1024 * 1024


def swapped(value):
    return lax.ppermute(value, "core", [(0, 1), (1, 0)])


def normalize(values, gain_row, shift_row):
    center = values - jnp.mean(values, -1, keepdims=True)
    spread = jnp.mean(center * center, -1, keepdims=True)
    return center * lax.rsqrt(spread + EPSILON) * gain_row + shift_row


def gelu_tanh(values):
    return jax.nn.gelu(values, approximate=True)


def contract(spec, left, right):
    return jnp.einsum(spec, left, right, preferred_element_type=F32)


def dot_over(left, right, left_dim, right_dim):
    return lax.dot_general(
        left, right, (((left_dim,), (right_dim,)), ((), ())), preferred_element_type=F32
    )


def scaled(block):
    return (block.astype(F32) * SCALE).astype(BF16)


def forward_kernel(z_ref, q_ref, k_ref, v_ref, row_ref, col_ref, out_ref, lse_ref, bias):
    keys, queries = bias.shape

    @pl.when(pl.program_id(0) == 0)
    def _():
        key_pos = lax.broadcasted_iota(jnp.int32, (keys, queries), 0)
        query_pos = z_ref[0] * queries + lax.broadcasted_iota(jnp.int32, (keys, queries), 1)
        docs = row_ref[z_ref[0]]
        same = col_ref[...].reshape(keys, 1) == docs
        bias[...] = jnp.where((key_pos <= query_pos) & same, 0.0, MASKED)

    scores = dot_over(k_ref[...], scaled(q_ref[...]), 0, 0) + bias[...]
    row_max = jnp.max(scores, 0, keepdims=True)
    powers = jnp.exp(scores - row_max)
    total = jnp.sum(powers, 0, keepdims=True)
    out = dot_over(v_ref[...], powers.astype(BF16), 1, 0) / total
    out_ref[...] = out.astype(BF16)
    lse_ref[0] = row_max + jnp.log(total)


def backward_kernel(
    z_ref, q_own, k_own, v_own, q_ref, k_ref, v_ref, do_ref, lse_ref, delta_ref,
    row_ref, col_ref, grad_ref, bias, dq, dk, dv,
):
    blocks, rows, _ = bias.shape
    z = z_ref[0]

    @pl.when(pl.program_id(0) == 0)
    def _():
        for j in range(blocks):

            @pl.when(j < z)
            def _():
                bias[j] = jnp.where(col_ref[j] == row_ref[z], 0.0, MASKED)

            @pl.when(j > z)
            def _():
                bias[j] = jnp.where(col_ref[z] == row_ref[j], 0.0, MASKED)

            @pl.when(j == z)
            def _():
                key_pos = lax.broadcasted_iota(jnp.int32, (rows, rows), 0)
                query_pos = lax.broadcasted_iota(jnp.int32, (rows, rows), 1)
                same = col_ref[z] == row_ref[z]
                bias[j] = jnp.where((key_pos <= query_pos) & same, 0.0, MASKED)

    query = scaled(q_own[...])
    key = k_own[...]
    value = v_own[...]
    d_out = do_ref[z]
    lse = lse_ref[z, 0]
    delta = delta_ref[z, 0]

    def pair(key_t, value_t, query_t, d_out_t, lse_row, delta_row, bias_block):
        scores = dot_over(key_t, query_t, 0, 0) + bias_block
        prob = jnp.exp(scores - lse_row)
        d_prob = dot_over(value_t, d_out_t, 0, 0)
        d_raw = (prob * (d_prob - delta_row)).astype(BF16)
        return prob.astype(BF16), d_raw

    prob, d_raw = pair(key, value, query, d_out, lse, delta, bias[z])
    dq[...] = dot_over(key, d_raw, 1, 0)
    dk[...] = dot_over(query, d_raw, 1, 1)
    dv[...] = dot_over(d_out, prob, 1, 1)

    for j in range(blocks):
        here = slice(j * rows, (j + 1) * rows)

        @pl.when(j < z)
        def _():
            key_j = k_ref[:, here]
            _, raw_j = pair(key_j, v_ref[:, here], query, d_out, lse, delta, bias[j])
            dq[...] += dot_over(key_j, raw_j, 1, 0)

        @pl.when(j > z)
        def _():
            query_j = scaled(q_ref[:, here])
            d_out_j = do_ref[j]
            prob_j, raw_j = pair(key, value, query_j, d_out_j, lse_ref[j, 0], delta_ref[j, 0], bias[j])
            dk[...] += dot_over(query_j, raw_j, 1, 1)
            dv[...] += dot_over(d_out_j, prob_j, 1, 1)

    grad_ref[0] = (dq[...] * SCALE).astype(BF16)
    grad_ref[1] = dk[...].astype(BF16)
    grad_ref[2] = dv[...].astype(BF16)


def whole_block(array):
    return pl.BlockSpec(array.shape, lambda h, z: (0,) * array.ndim)


def head_specs(rows, length):
    own = [
        pl.BlockSpec((HEAD_DIM, rows), functools.partial(lambda p, h, z: (p * HEADS + h, z[0]), p))
        for p in range(3)
    ]
    full = [
        pl.BlockSpec((HEAD_DIM, length), functools.partial(lambda p, h, z: (p * HEADS + h, 0), p))
        for p in range(3)
    ]
    return own, full


def attend(z_index, joined_t, seg_rows, seg_cols, rows):
    length = joined_t.shape[1]
    own, full = head_specs(rows, length)
    return pl.pallas_call(
        forward_kernel,
        grid_spec=pltpu.PrefetchScalarGridSpec(
            num_scalar_prefetch=1,
            grid=(HEADS,),
            in_specs=[own[0], full[1], full[2], whole_block(seg_rows), whole_block(seg_cols)],
            out_specs=[
                pl.BlockSpec((HEAD_DIM, rows), lambda h, z: (h, 0)),
                pl.BlockSpec((1, 1, rows), lambda h, z: (h, 0, 0)),
            ],
            scratch_shapes=[pltpu.VMEM((length, rows), F32)],
        ),
        out_shape=[
            jax.ShapeDtypeStruct((HEADS * HEAD_DIM, rows), BF16),
            jax.ShapeDtypeStruct((HEADS, 1, rows), F32),
        ],
        compiler_params=pltpu.CompilerParams(vmem_limit_bytes=VMEM_BYTES),
        cost_estimate=pl.CostEstimate(
            flops=4 * HEADS * HEAD_DIM * rows * length,
            bytes_accessed=4 * HEADS * HEAD_DIM * length,
            transcendentals=HEADS * rows * length,
        ),
        name="attend",
    )(z_index, joined_t, joined_t, joined_t, seg_rows, seg_cols)


def attend_back(z_index, joined_t, d_att_all, lse_all, delta_all, seg_rows, seg_cols, rows):
    length = joined_t.shape[1]
    blocks = length // rows
    own, full = head_specs(rows, length)
    row_spec = pl.BlockSpec((blocks, 1, 1, rows), lambda h, z: (0, h, 0, 0))
    return pl.pallas_call(
        backward_kernel,
        grid_spec=pltpu.PrefetchScalarGridSpec(
            num_scalar_prefetch=1,
            grid=(HEADS,),
            in_specs=own
            + full
            + [
                pl.BlockSpec((blocks, HEAD_DIM, rows), lambda h, z: (0, h, 0)),
                row_spec,
                row_spec,
                whole_block(seg_rows),
                whole_block(seg_cols),
            ],
            out_specs=pl.BlockSpec((3, HEAD_DIM, rows), lambda h, z: (0, h, 0)),
            scratch_shapes=[pltpu.VMEM((blocks, rows, rows), F32)]
            + [pltpu.VMEM((HEAD_DIM, rows), F32)] * 3,
        ),
        out_shape=jax.ShapeDtypeStruct((3, HEADS * HEAD_DIM, rows), BF16),
        compiler_params=pltpu.CompilerParams(vmem_limit_bytes=VMEM_BYTES),
        cost_estimate=pl.CostEstimate(
            flops=8 * HEADS * HEAD_DIM * rows * length,
            bytes_accessed=8 * HEADS * HEAD_DIM * length,
            transcendentals=HEADS * rows * length,
        ),
        name="attend_back",
    )(z_index, *([joined_t] * 6), d_att_all, lse_all, delta_all, seg_rows, seg_cols)


def local(
    inputs,
    segments,
    ln1_gain,
    ln1_bias,
    qkv_weight,
    query_bias,
    value_bias,
    proj_weight,
    proj_bias,
    ln2_gain,
    ln2_bias,
    fc_weight,
    fc_bias,
    out_weight,
    out_bias,
    cotangent,
):
    part, seqs, width = inputs.shape
    dp, nz = lax.axis_size("dp"), lax.axis_size("z")
    z, core = lax.axis_index("z"), lax.axis_index("core")
    rows = 2 * part
    shard_rows, qkv_cols = qkv_weight.shape
    proj_cols = proj_weight.shape[1]
    units = fc_weight.shape[1]
    first = core == 0

    seg_row = jnp.pad(segments.reshape(1, seqs * part).astype(BF16), ((0, 7), (0, width - seqs * part)))
    packed = jnp.concatenate(
        [inputs[:, 0], inputs[:, 1], cotangent[:, 0], cotangent[:, 1], seg_row], 0
    )
    arrived = swapped(packed)
    low_part = jnp.where(first, packed, arrived)
    high_part = jnp.where(first, arrived, packed)

    def chip_rows(slot):
        here = slice(slot * part, (slot + 1) * part)
        return jnp.concatenate([low_part[here], high_part[here]], 0)

    def own_other(slot):
        zero, one = chip_rows(slot), chip_rows(slot + 1)
        return jnp.where(first, zero, one), jnp.where(first, one, zero)

    x_own, x_other = own_other(0)
    g_own, g_other = own_other(2)
    segs = [
        jnp.concatenate(
            [low_part[4 * part, i * part : (i + 1) * part], high_part[4 * part, i * part : (i + 1) * part]]
        )
        for i in range(2)
    ]
    seg_own = jnp.pad(jnp.where(first, segs[0], segs[1]).reshape(1, rows), ((0, 7), (0, width - rows)))

    bias_row = jnp.pad(fc_bias.reshape(1, units), ((0, 7), (0, qkv_cols + proj_cols - units)))
    pair_block = jnp.concatenate([jnp.concatenate([qkv_weight, proj_weight], 1), bias_row], 0)
    pair_half = lax.all_gather(pair_block, GROUP, axis=0, tiled=False)
    seq_all = lax.all_gather(jnp.concatenate([x_own, seg_own], 0), "z", axis=0, tiled=False)
    w_fc = lax.all_gather(fc_weight.T, GROUP, axis=0, tiled=True)
    w_out = lax.all_gather(out_weight, GROUP, axis=0, tiled=True)
    b_fc = pair_half[:, shard_rows, :units].reshape(-1).astype(F32)
    pair_mine = pair_half[:, :shard_rows]
    pair_other = swapped(pair_mine)
    pair_full = jnp.stack(
        [jnp.where(first, pair_mine, pair_other), jnp.where(first, pair_other, pair_mine)]
    ).reshape(2, dp, nz, shard_rows, qkv_cols + proj_cols)
    pair_full = jnp.transpose(pair_full, (2, 0, 3, 1, 4)).reshape(width, dp, qkv_cols + proj_cols)
    w_qkv = pair_full[..., :qkv_cols].reshape(width, dp * qkv_cols)
    w_proj = pair_full[..., qkv_cols:].reshape(width, dp * proj_cols)

    x_all = seq_all[:, :rows].reshape(nz * rows, width)
    docs = seq_all[:, rows, :rows].astype(F32)
    seg_rows, seg_cols = docs.reshape(nz, 1, rows), docs.reshape(nz, rows, 1)
    z_index = z.astype(jnp.int32).reshape(1)

    h1_all = normalize(x_all.astype(F32), ln1_gain, ln1_bias).astype(BF16)
    qkv_bias = jnp.concatenate([query_bias, jnp.zeros_like(query_bias), value_bias])
    joined_t = (contract("dn,rd->nr", w_qkv, h1_all) + qkv_bias[:, None]).astype(BF16)
    att_t, lse = attend(z_index, joined_t, seg_rows, seg_cols, rows)
    lse_all = lax.all_gather(lse, "z", axis=0, tiled=False)
    att_other_t = swapped(att_t)

    x_f = x_own.astype(F32)
    resid = x_f + contract("dr,dn->rn", att_t, w_proj) + proj_bias
    h2_f, ln2_back = jax.vjp(normalize, resid, ln2_gain, ln2_bias)
    h2 = h2_f.astype(BF16)
    h2_other = swapped(h2)

    def hidden(rows_in, gradient):
        pre = contract("rd,nd->rn", rows_in, w_fc) + b_fc
        act, gelu_back = jax.vjp(gelu_tanh, pre)
        d_pre = gelu_back(contract("rd,nd->rn", gradient, w_out))[0]
        return act.astype(BF16), d_pre.astype(BF16)

    act, d_pre = hidden(h2, g_own)
    act_other, d_pre_other = hidden(h2_other, g_other)
    d_h2_sent = swapped(contract("rn,nd->rd", d_pre_other, w_fc).astype(BF16))
    y_sent = swapped(contract("rn,nd->rd", act_other, w_out).astype(BF16))
    d_h2 = contract("rn,nd->rd", d_pre, w_fc) + d_h2_sent.astype(F32)
    output = (resid + contract("rn,nd->rd", act, w_out) + y_sent.astype(F32) + out_bias).astype(BF16)

    def scattered(blocks):
        return lax.psum_scatter(blocks.astype(BF16), GROUP, scatter_dimension=0, tiled=True)

    out_grad = scattered(
        contract("rn,rd->nd", act, g_own) + contract("rn,rd->nd", act_other, g_other)
    )
    fc_grad = scattered(
        contract("rn,rd->nd", d_pre, h2) + contract("rn,rd->nd", d_pre_other, h2_other)
    )
    d_resid_part, ln2_gain_grad, ln2_bias_grad = ln2_back(d_h2)
    d_resid = g_own.astype(F32) + d_resid_part
    d_branch = d_resid.astype(BF16)
    d_branch_other = swapped(d_branch)
    d_att_t = contract("rn,dn->dr", d_branch, w_proj).astype(BF16)
    products = d_att_t.astype(F32) * att_t.astype(F32)
    delta = jnp.sum(products.reshape(HEADS, HEAD_DIM, rows), 1, keepdims=True)
    d_att_all = lax.all_gather(d_att_t, "z", axis=0, tiled=False)
    delta_all = lax.all_gather(delta, "z", axis=0, tiled=False)

    fc_bias_part = jnp.sum(d_pre.astype(F32), 0) + jnp.sum(d_pre_other.astype(F32), 0)
    early = jnp.concatenate(
        [
            jnp.sum(g_own.astype(F32), 0),
            jnp.sum(d_branch.astype(F32), 0),
            ln2_gain_grad,
            ln2_bias_grad,
            fc_bias_part,
        ]
    ).reshape(1, -1)
    early_all = lax.all_gather(early, EVERY, axis=0, tiled=True)
    early_sum = jnp.sum(early_all[:, : 4 * width], 0).reshape(4, width)
    fc_parts = early_all[:, 4 * width :].reshape(dp * nz, 2, dp * nz, units)
    fc_parts = lax.dynamic_index_in_dim(fc_parts, core, 1, keepdims=False)
    place = lax.axis_index("dp") * nz + z
    fc_bias_grad = jnp.sum(lax.dynamic_index_in_dim(fc_parts, place, 1, keepdims=False), 0)

    grads_t = attend_back(z_index, joined_t, d_att_all, lse_all, delta_all, seg_rows, seg_cols, rows)
    dj_t = grads_t.reshape(3 * width, rows)
    dj_other_t = swapped(dj_t)

    def my_columns(block):
        split = block.reshape(block.shape[0], nz, 2, shard_rows)
        return jnp.where(first, split[:, :, 0], split[:, :, 1]).reshape(block.shape[0], -1)

    def my_rows(block_t):
        split = block_t.reshape(nz, 2, shard_rows, block_t.shape[1])
        return jnp.where(first, split[:, 0], split[:, 1]).reshape(-1, block_t.shape[1])

    h1_own = normalize(x_f, ln1_gain, ln1_bias).astype(BF16)
    h1_other = normalize(x_other.astype(F32), ln1_gain, ln1_bias).astype(BF16)
    h1_mine, h1_mine_other = my_columns(h1_own), my_columns(h1_other)
    att_mine, att_mine_other = my_rows(att_t), my_rows(att_other_t)
    pair_parts = []
    for i in range(dp):
        take = slice(i * qkv_cols, (i + 1) * qkv_cols)
        qkv_part = contract("ra,nr->an", h1_mine, dj_t[take]) + contract(
            "ra,nr->an", h1_mine_other, dj_other_t[take]
        )
        take = slice(i * proj_cols, (i + 1) * proj_cols)
        proj_part = contract("ar,rn->an", att_mine, d_branch[:, take]) + contract(
            "ar,rn->an", att_mine_other, d_branch_other[:, take]
        )
        pair_parts.append(jnp.concatenate([qkv_part.astype(BF16), proj_part.astype(BF16)], 1))
    pair_grad = scattered(jnp.concatenate(pair_parts, 0))

    _, ln1_back = jax.vjp(normalize, x_f, ln1_gain, ln1_bias)
    d_normed = contract("nr,dn->rd", dj_t, w_qkv)
    d_input_part, ln1_gain_grad, ln1_bias_grad = ln1_back(d_normed)
    input_grad = (d_resid + d_input_part).astype(BF16)
    dj_sums = jnp.sum(dj_t.astype(F32), 1)
    late = jnp.concatenate(
        [ln1_gain_grad, ln1_bias_grad, dj_sums[:width], dj_sums[2 * width :]]
    ).reshape(1, -1)
    late_sum = jnp.sum(lax.all_gather(late, EVERY, axis=0, tiled=True), 0).reshape(4, width)

    def placed(block):
        mine = jnp.where(first, block[:part], block[part:])
        sent = swapped(jnp.where(first, block[part:], block[:part]))
        return jnp.stack([jnp.where(first, mine, sent), jnp.where(first, sent, mine)], 1)

    return (
        placed(output),
        placed(input_grad),
        late_sum[0],
        late_sum[1],
        pair_grad[:, :qkv_cols].astype(F32),
        late_sum[2],
        late_sum[3],
        pair_grad[:, qkv_cols:].astype(F32),
        early_sum[1],
        early_sum[2],
        early_sum[3],
        fc_grad.astype(F32).T,
        fc_bias_grad,
        out_grad.astype(F32),
        early_sum[0],
    )


def solution(mesh):
    dp, ctx = mesh.shape["dp"], mesh.shape["ctx"]
    split = Mesh(mesh.devices.reshape(dp, ctx // 2, 2), EVERY)
    ctx_axes = ("z", "core")
    tokens = P(ctx_axes, "dp", None)
    pair = P(ctx_axes, "dp")
    columns, units, unit_rows = P(None, EVERY), P(EVERY), P(EVERY, None)
    return jax.shard_map(
        local,
        mesh=split,
        in_specs=(
            tokens, P("dp", ctx_axes), P(), P(), pair, P(), P(), pair,
            P(), P(), P(), columns, units, unit_rows, P(), tokens,
        ),
        out_specs=(
            tokens, tokens, P(), P(), pair, P(), P(), pair,
            P(), P(), P(), columns, units, unit_rows, P(),
        ),
        check_vma=False,
    )
```

```python
import functools

import jax
import jax.numpy as jnp
from jax import lax
from jax.experimental import pallas as pl
from jax.experimental.pallas import tpu as pltpu
from jax.sharding import Mesh
from jax.sharding import PartitionSpec as P

HEADS = 17
HEAD_DIM = 64
EPSILON = 1e-05
MASKED = -1e30
SCALE = HEAD_DIM ** (-0.5)
GROUP = ("dp", "z")
EVERY = ("dp", "z", "core")
BF16 = jnp.bfloat16
F32 = jnp.float32
VMEM_BYTES = 48 * 1024 * 1024


def swapped(value):
    return lax.ppermute(value, "core", [(0, 1), (1, 0)])


def exchanged(value, axis, bit):
    return lax.ppermute(value, axis, [(i, i ^ bit) for i in range(lax.axis_size(axis))])


def axis_bits(axis):
    size = lax.axis_size(axis)
    return [(axis, 1 << b) for b in reversed(range(size.bit_length() - 1))]


def doubled(block, order):
    bits = axis_bits("dp") + axis_bits("z")
    held = block.reshape((1,) * len(bits) + block.shape)
    for place in order:
        held = jnp.concatenate([held, exchanged(held, *bits[place])], place)
    return held.reshape((-1,) + block.shape)


def halved(blocks, order):
    bits = axis_bits("dp") + axis_bits("z")
    block_shape = blocks.shape[1:]
    held = blocks.astype(BF16).reshape((2,) * len(bits) + block_shape)
    for place in order:
        keep = lax.slice_in_dim(held, 0, 1, axis=place)
        sent = exchanged(lax.slice_in_dim(held, 1, 2, axis=place), *bits[place])
        held = (keep.astype(F32) + sent.astype(F32)).astype(BF16)
    return held.reshape(block_shape)


def along_z(block):
    bits = axis_bits("z")
    held = block.reshape((1,) * len(bits) + block.shape)
    for place in range(len(bits)):
        held = jnp.concatenate([held, exchanged(held, *bits[place])], place)
    return held.reshape((-1,) + block.shape)


def summed_everywhere(value):
    for axis, bit in [("core", 1)] + axis_bits("z") + axis_bits("dp"):
        value = value + exchanged(value, axis, bit)
    return value


def reorder_kernel(take_ref, low_mine, high_mine, low_other, high_other, out_ref):
    rows, cut = out_ref.shape[1], low_mine.shape[1]
    mine = pl.program_id(0) % 2 == take_ref[take_ref.shape[0] - 1]

    def put(low_ref, high_ref):
        out_ref[0, :cut] = low_ref[0]
        out_ref[0, cut:] = high_ref[0, : rows - cut]

    @pl.when(mine)
    def _():
        put(low_mine, high_mine)

    @pl.when(jnp.logical_not(mine))
    def _():
        put(low_other, high_other)


def reorder_weights(take, low_mine, high_mine, low_other, high_other, rows):
    count, _, width = low_mine.shape

    def taken(array):
        return pl.BlockSpec((1,) + array.shape[1:], lambda i, t: (t[i // 2], 0, 0))

    parts = (low_mine, high_mine, low_other, high_other)
    return pl.pallas_call(
        reorder_kernel,
        grid_spec=pltpu.PrefetchScalarGridSpec(
            num_scalar_prefetch=1,
            grid=(2 * count,),
            in_specs=[taken(array) for array in parts],
            out_specs=pl.BlockSpec((1, rows, width), lambda i, t: (i, 0, 0)),
        ),
        out_shape=jax.ShapeDtypeStruct((2 * count, rows, width), BF16),
        compiler_params=pltpu.CompilerParams(vmem_limit_bytes=VMEM_BYTES),
        cost_estimate=pl.CostEstimate(flops=0, bytes_accessed=12 * count * rows * width, transcendentals=0),
        name="reorder_weights",
    )(take, *parts)


def copy_kernel(take_ref, in_ref, out_ref):
    out_ref[...] = in_ref[...]


def reorder_blocks(take, blocks):
    count, rows, width = blocks.shape
    return pl.pallas_call(
        copy_kernel,
        grid_spec=pltpu.PrefetchScalarGridSpec(
            num_scalar_prefetch=1,
            grid=(count,),
            in_specs=[pl.BlockSpec((1, rows, width), lambda i, t: (t[i], 0, 0))],
            out_specs=pl.BlockSpec((1, rows, width), lambda i, t: (i, 0, 0)),
        ),
        out_shape=jax.ShapeDtypeStruct(blocks.shape, BF16),
        compiler_params=pltpu.CompilerParams(vmem_limit_bytes=VMEM_BYTES),
        cost_estimate=pl.CostEstimate(flops=0, bytes_accessed=4 * count * rows * width, transcendentals=0),
        name="reorder_blocks",
    )(take, blocks)


def normalize(values, gain_row, shift_row):
    center = values - jnp.mean(values, -1, keepdims=True)
    spread = jnp.mean(center * center, -1, keepdims=True)
    return center * lax.rsqrt(spread + EPSILON) * gain_row + shift_row


def gelu_tanh(values):
    return jax.nn.gelu(values, approximate=True)


def contract(spec, left, right):
    return jnp.einsum(spec, left, right, preferred_element_type=F32)


def dot_over(left, right, left_dim, right_dim):
    return lax.dot_general(
        left, right, (((left_dim,), (right_dim,)), ((), ())), preferred_element_type=F32
    )


def scaled(block):
    return (block.astype(F32) * SCALE).astype(BF16)


def forward_kernel(z_ref, q_ref, k_ref, v_ref, row_ref, col_ref, out_ref, lse_ref, bias):
    keys, queries = bias.shape

    @pl.when(pl.program_id(0) == 0)
    def _():
        key_pos = lax.broadcasted_iota(jnp.int32, (keys, queries), 0)
        query_pos = z_ref[0] * queries + lax.broadcasted_iota(jnp.int32, (keys, queries), 1)
        docs = row_ref[z_ref[0]]
        same = col_ref[...].reshape(keys, 1) == docs
        bias[...] = jnp.where((key_pos <= query_pos) & same, 0.0, MASKED)

    scores = dot_over(k_ref[...], scaled(q_ref[...]), 0, 0) + bias[...]
    row_max = jnp.max(scores, 0, keepdims=True)
    powers = jnp.exp(scores - row_max)
    total = jnp.sum(powers, 0, keepdims=True)
    out = dot_over(v_ref[...], powers.astype(BF16), 1, 0) / total
    out_ref[...] = out.astype(BF16)
    lse_ref[0] = row_max + jnp.log(total)


def backward_kernel(
    z_ref, q_own, k_own, v_own, q_ref, k_ref, v_ref, do_ref, lse_ref, delta_ref,
    row_ref, col_ref, grad_ref, bias, dq, dk, dv,
):
    blocks, rows, _ = bias.shape
    z = z_ref[0]

    @pl.when(pl.program_id(0) == 0)
    def _():
        for j in range(blocks):

            @pl.when(j < z)
            def _():
                bias[j] = jnp.where(col_ref[j] == row_ref[z], 0.0, MASKED)

            @pl.when(j > z)
            def _():
                bias[j] = jnp.where(col_ref[z] == row_ref[j], 0.0, MASKED)

            @pl.when(j == z)
            def _():
                key_pos = lax.broadcasted_iota(jnp.int32, (rows, rows), 0)
                query_pos = lax.broadcasted_iota(jnp.int32, (rows, rows), 1)
                same = col_ref[z] == row_ref[z]
                bias[j] = jnp.where((key_pos <= query_pos) & same, 0.0, MASKED)

    query = scaled(q_own[...])
    key = k_own[...]
    value = v_own[...]
    d_out = do_ref[0]
    lse = lse_ref[0, 0]
    delta = delta_ref[0, 0]

    def pair(key_t, value_t, query_t, d_out_t, lse_row, delta_row, bias_block):
        scores = dot_over(key_t, query_t, 0, 0) + bias_block
        prob = jnp.exp(scores - lse_row)
        d_prob = dot_over(value_t, d_out_t, 0, 0)
        d_raw = (prob * (d_prob - delta_row)).astype(BF16)
        return prob.astype(BF16), d_raw

    prob, d_raw = pair(key, value, query, d_out, lse, delta, bias[z])
    dq[...] = dot_over(key, d_raw, 1, 0)
    dk[...] = dot_over(query, d_raw, 1, 1)
    dv[...] = dot_over(d_out, prob, 1, 1)

    for j in range(blocks):
        here = slice(j * rows, (j + 1) * rows)

        @pl.when(j < z)
        def _():
            key_j = k_ref[:, here]
            _, raw_j = pair(key_j, v_ref[:, here], query, d_out, lse, delta, bias[j])
            dq[...] += dot_over(key_j, raw_j, 1, 0)

        @pl.when(j > z)
        def _():
            query_j = scaled(q_ref[:, here])
            slot = jnp.bitwise_xor(z, j)
            d_out_j = do_ref[slot]
            prob_j, raw_j = pair(
                key, value, query_j, d_out_j, lse_ref[slot, 0], delta_ref[slot, 0], bias[j]
            )
            dk[...] += dot_over(query_j, raw_j, 1, 1)
            dv[...] += dot_over(d_out_j, prob_j, 1, 1)

    grad_ref[0] = (dq[...] * SCALE).astype(BF16)
    grad_ref[1] = dk[...].astype(BF16)
    grad_ref[2] = dv[...].astype(BF16)


def whole_block(array):
    return pl.BlockSpec(array.shape, lambda h, z: (0,) * array.ndim)


def head_specs(rows, length):
    own = [
        pl.BlockSpec((HEAD_DIM, rows), functools.partial(lambda p, h, z: (p * HEADS + h, z[0]), p))
        for p in range(3)
    ]
    full = [
        pl.BlockSpec((HEAD_DIM, length), functools.partial(lambda p, h, z: (p * HEADS + h, 0), p))
        for p in range(3)
    ]
    return own, full


def attend(z_index, joined_t, seg_rows, seg_cols, rows):
    length = joined_t.shape[1]
    own, full = head_specs(rows, length)
    return pl.pallas_call(
        forward_kernel,
        grid_spec=pltpu.PrefetchScalarGridSpec(
            num_scalar_prefetch=1,
            grid=(HEADS,),
            in_specs=[own[0], full[1], full[2], whole_block(seg_rows), whole_block(seg_cols)],
            out_specs=[
                pl.BlockSpec((HEAD_DIM, rows), lambda h, z: (h, 0)),
                pl.BlockSpec((1, 1, rows), lambda h, z: (h, 0, 0)),
            ],
            scratch_shapes=[pltpu.VMEM((length, rows), F32)],
        ),
        out_shape=[
            jax.ShapeDtypeStruct((HEADS * HEAD_DIM, rows), BF16),
            jax.ShapeDtypeStruct((HEADS, 1, rows), F32),
        ],
        compiler_params=pltpu.CompilerParams(vmem_limit_bytes=VMEM_BYTES),
        cost_estimate=pl.CostEstimate(
            flops=4 * HEADS * HEAD_DIM * rows * length,
            bytes_accessed=4 * HEADS * HEAD_DIM * length,
            transcendentals=HEADS * rows * length,
        ),
        name="attend",
    )(z_index, joined_t, joined_t, joined_t, seg_rows, seg_cols)


def attend_back(z_index, joined_t, d_att_all, lse_all, delta_all, seg_rows, seg_cols, rows):
    length = joined_t.shape[1]
    blocks = length // rows
    own, full = head_specs(rows, length)
    row_spec = pl.BlockSpec((blocks, 1, 1, rows), lambda h, z: (0, h, 0, 0))
    return pl.pallas_call(
        backward_kernel,
        grid_spec=pltpu.PrefetchScalarGridSpec(
            num_scalar_prefetch=1,
            grid=(HEADS,),
            in_specs=own
            + full
            + [
                pl.BlockSpec((blocks, HEAD_DIM, rows), lambda h, z: (0, h, 0)),
                row_spec,
                row_spec,
                whole_block(seg_rows),
                whole_block(seg_cols),
            ],
            out_specs=pl.BlockSpec((3, HEAD_DIM, rows), lambda h, z: (0, h, 0)),
            scratch_shapes=[pltpu.VMEM((blocks, rows, rows), F32)]
            + [pltpu.VMEM((HEAD_DIM, rows), F32)] * 3,
        ),
        out_shape=jax.ShapeDtypeStruct((3, HEADS * HEAD_DIM, rows), BF16),
        compiler_params=pltpu.CompilerParams(vmem_limit_bytes=VMEM_BYTES),
        cost_estimate=pl.CostEstimate(
            flops=8 * HEADS * HEAD_DIM * rows * length,
            bytes_accessed=8 * HEADS * HEAD_DIM * length,
            transcendentals=HEADS * rows * length,
        ),
        name="attend_back",
    )(z_index, *([joined_t] * 6), d_att_all, lse_all, delta_all, seg_rows, seg_cols)


def local(
    inputs,
    segments,
    ln1_gain,
    ln1_bias,
    qkv_weight,
    query_bias,
    value_bias,
    proj_weight,
    proj_bias,
    ln2_gain,
    ln2_bias,
    fc_weight,
    fc_bias,
    out_weight,
    out_bias,
    cotangent,
):
    part, seqs, width = inputs.shape
    dp, nz = lax.axis_size("dp"), lax.axis_size("z")
    z, core = lax.axis_index("z"), lax.axis_index("core")
    rows = 2 * part
    shard_rows, qkv_cols = qkv_weight.shape
    proj_cols = proj_weight.shape[1]
    units = fc_weight.shape[1]
    first = core == 0

    seg_row = jnp.pad(segments.reshape(1, seqs * part).astype(BF16), ((0, 7), (0, width - seqs * part)))
    packed = jnp.concatenate(
        [inputs[:, 0], inputs[:, 1], cotangent[:, 0], cotangent[:, 1], seg_row], 0
    )
    arrived = swapped(packed)
    low_part = jnp.where(first, packed, arrived)
    high_part = jnp.where(first, arrived, packed)

    def chip_rows(slot):
        here = slice(slot * part, (slot + 1) * part)
        return jnp.concatenate([low_part[here], high_part[here]], 0)

    def own_other(slot):
        zero, one = chip_rows(slot), chip_rows(slot + 1)
        return jnp.where(first, zero, one), jnp.where(first, one, zero)

    x_own, x_other = own_other(0)
    g_own, g_other = own_other(2)
    segs = [
        jnp.concatenate(
            [low_part[4 * part, i * part : (i + 1) * part], high_part[4 * part, i * part : (i + 1) * part]]
        )
        for i in range(2)
    ]
    seg_own = jnp.pad(jnp.where(first, segs[0], segs[1]).reshape(1, rows), ((0, 7), (0, width - rows)))

    bias_row = jnp.pad(fc_bias.reshape(1, units), ((0, 7), (0, qkv_cols + proj_cols - units)))
    pair_block = jnp.concatenate([jnp.concatenate([qkv_weight, proj_weight], 1), bias_row], 0)
    seq_all = lax.all_gather(jnp.concatenate([x_own, seg_own], 0), "z", axis=0, tiled=False)
    dp_places = list(range(dp.bit_length() - 1))
    z_places = [len(dp_places) + i for i in range(nz.bit_length() - 1)]
    grow = z_places + dp_places, z_places + dp_places[::-1]
    shrink = dp_places + z_places[::-1], dp_places[::-1] + z_places[::-1]
    take = (
        (jnp.arange(dp)[:, None] ^ lax.axis_index("dp")) * nz + (jnp.arange(nz)[None] ^ z)
    ).reshape(-1).astype(jnp.int32)
    cut = pair_block.shape[0] // 32 * 16
    low_half = doubled(pair_block[:cut], grow[0])
    high_half = doubled(pair_block[cut:], grow[1])
    out_block, low_half, high_half = lax.optimization_barrier((out_weight, low_half, high_half))
    w_out = doubled(out_block, grow[1]).reshape(-1, width)
    fc_block, seq_all = lax.optimization_barrier((fc_weight.T, seq_all))
    w_fc = lax.all_gather(fc_block, GROUP, axis=0, tiled=False)
    w_fc = reorder_blocks(take, w_fc)
    w_fc = w_fc.reshape(-1, width)
    b_fc = high_half[:, shard_rows - cut, :units].reshape(-1).astype(F32)
    w_pair = reorder_weights(
        jnp.concatenate([take, core.astype(jnp.int32).reshape(1)]),
        low_half,
        high_half,
        swapped(low_half),
        swapped(high_half),
        shard_rows,
    ).reshape(dp, width, qkv_cols + proj_cols)
    w_qkv, w_proj = w_pair[..., :qkv_cols], w_pair[..., qkv_cols:]

    x_all = seq_all[:, :rows].reshape(nz * rows, width)
    docs = seq_all[:, rows, :rows].astype(F32)
    seg_rows, seg_cols = docs.reshape(nz, 1, rows), docs.reshape(nz, rows, 1)
    z_index = z.astype(jnp.int32).reshape(1)

    h1_all = normalize(x_all.astype(F32), ln1_gain, ln1_bias).astype(BF16)
    qkv_bias = jnp.concatenate([query_bias, jnp.zeros_like(query_bias), value_bias])
    joined_t = (contract("cdn,rd->cnr", w_qkv, h1_all).reshape(3 * width, -1) + qkv_bias[:, None]).astype(BF16)
    att_t, lse = attend(z_index, joined_t, seg_rows, seg_cols, rows)
    lse_all = along_z(lse)
    att_other_t = swapped(att_t)

    x_f = x_own.astype(F32)
    branch = [contract("dr,dn->rn", att_t, w_proj[i]) for i in range(dp)]
    resid = x_f + jnp.concatenate(branch, 1) + proj_bias
    h2_f, ln2_back = jax.vjp(normalize, resid, ln2_gain, ln2_bias)
    h2 = h2_f.astype(BF16)
    h2_other = swapped(h2)

    def hidden(rows_in, gradient):
        pre = contract("rd,nd->rn", rows_in, w_fc) + b_fc
        act, gelu_back = jax.vjp(gelu_tanh, pre)
        d_pre = gelu_back(contract("rd,nd->rn", gradient, w_out))[0]
        return act.astype(BF16), d_pre.astype(BF16)

    act, d_pre = hidden(h2, g_own)
    act_other, d_pre_other = hidden(h2_other, g_other)
    d_h2_sent = swapped(contract("rn,nd->rd", d_pre_other, w_fc).astype(BF16))
    y_sent = swapped(contract("rn,nd->rd", act_other, w_out).astype(BF16))
    d_h2 = contract("rn,nd->rd", d_pre, w_fc) + d_h2_sent.astype(F32)
    output = (resid + contract("rn,nd->rd", act, w_out) + y_sent.astype(F32) + out_bias).astype(BF16)

    out_parts = contract("rn,rd->nd", act, g_own) + contract("rn,rd->nd", act_other, g_other)
    fc_parts = contract("rn,rd->nd", d_pre, h2) + contract("rn,rd->nd", d_pre_other, h2_other)
    out_grad = halved(out_parts.reshape(dp * nz, units, width), shrink[0])
    fc_grad = halved(fc_parts.reshape(dp * nz, units, width), shrink[1])
    d_resid_part, ln2_gain_grad, ln2_bias_grad = ln2_back(d_h2)
    d_resid = g_own.astype(F32) + d_resid_part
    d_branch = d_resid.astype(BF16)
    d_branch_other = swapped(d_branch)
    d_att_t = sum(
        contract("rn,dn->dr", d_branch[:, i * proj_cols : (i + 1) * proj_cols], w_proj[i])
        for i in range(dp)
    ).astype(BF16)
    products = d_att_t.astype(F32) * att_t.astype(F32)
    delta = jnp.sum(products.reshape(HEADS, HEAD_DIM, rows), 1, keepdims=True)
    d_att_all, delta_all = along_z(d_att_t), along_z(delta)

    fc_bias_part = jnp.sum(d_pre.astype(F32), 0) + jnp.sum(d_pre_other.astype(F32), 0)
    early_sum = summed_everywhere(
        jnp.stack([jnp.sum(g_own.astype(F32), 0), jnp.sum(d_branch.astype(F32), 0), ln2_gain_grad, ln2_bias_grad])
    )
    fc_bias_grad = fc_bias_part.reshape((dp, nz, units))
    for axis, dim in (("dp", 0), ("z", 1)):
        for _, bit in axis_bits(axis):
            keep = lax.slice_in_dim(fc_bias_grad, 0, bit, axis=dim)
            sent = lax.slice_in_dim(fc_bias_grad, bit, 2 * bit, axis=dim)
            fc_bias_grad = keep + exchanged(sent, axis, bit)
    fc_bias_grad = fc_bias_grad.reshape(units)

    grads_t = attend_back(z_index, joined_t, d_att_all, lse_all, delta_all, seg_rows, seg_cols, rows)
    dj_t = grads_t.reshape(3 * width, rows)
    dj_other_t = swapped(dj_t)

    def my_columns(block):
        split = block.reshape(block.shape[0], nz, 2, shard_rows)
        return jnp.where(first, split[:, :, 0], split[:, :, 1]).reshape(block.shape[0], -1)

    def my_rows(block_t):
        split = block_t.reshape(nz, 2, shard_rows, block_t.shape[1])
        return jnp.where(first, split[:, 0], split[:, 1]).reshape(-1, block_t.shape[1])

    h1_own = normalize(x_f, ln1_gain, ln1_bias).astype(BF16)
    h1_other = normalize(x_other.astype(F32), ln1_gain, ln1_bias).astype(BF16)
    h1_mine, h1_mine_other = my_columns(h1_own), my_columns(h1_other)
    att_mine, att_mine_other = my_rows(att_t), my_rows(att_other_t)
    pair_parts = []
    for i in range(dp):
        span = slice(i * qkv_cols, (i + 1) * qkv_cols)
        qkv_part = contract("ra,nr->an", h1_mine, dj_t[span]) + contract(
            "ra,nr->an", h1_mine_other, dj_other_t[span]
        )
        span = slice(i * proj_cols, (i + 1) * proj_cols)
        proj_part = contract("ar,rn->an", att_mine, d_branch[:, span]) + contract(
            "ar,rn->an", att_mine_other, d_branch_other[:, span]
        )
        pair_parts.append(jnp.concatenate([qkv_part.astype(BF16), proj_part.astype(BF16)], 1))
    pair_sent = reorder_blocks(
        take, jnp.concatenate(pair_parts, 0).reshape(dp * nz, shard_rows, qkv_cols + proj_cols)
    )
    pair_grad = jnp.concatenate(
        [halved(pair_sent[:, :cut], shrink[0]), halved(pair_sent[:, cut:], shrink[1])], 0
    )

    _, ln1_back = jax.vjp(normalize, x_f, ln1_gain, ln1_bias)
    d_normed = sum(
        contract("nr,dn->rd", dj_t[i * qkv_cols : (i + 1) * qkv_cols], w_qkv[i]) for i in range(dp)
    )
    d_input_part, ln1_gain_grad, ln1_bias_grad = ln1_back(d_normed)
    input_grad = (d_resid + d_input_part).astype(BF16)
    dj_sums = jnp.sum(dj_t.astype(F32), 1)
    late_sum = summed_everywhere(
        jnp.stack([ln1_gain_grad, ln1_bias_grad, dj_sums[:width], dj_sums[2 * width :]])
    )

    def placed(block):
        mine = jnp.where(first, block[:part], block[part:])
        sent = swapped(jnp.where(first, block[part:], block[:part]))
        return jnp.stack([jnp.where(first, mine, sent), jnp.where(first, sent, mine)], 1)

    return (
        placed(output),
        placed(input_grad),
        late_sum[0],
        late_sum[1],
        pair_grad[:, :qkv_cols].astype(F32),
        late_sum[2],
        late_sum[3],
        pair_grad[:, qkv_cols:].astype(F32),
        early_sum[1],
        early_sum[2],
        early_sum[3],
        fc_grad.astype(F32).T,
        fc_bias_grad,
        out_grad.astype(F32),
        early_sum[0],
    )


def solution(mesh):
    dp, ctx = mesh.shape["dp"], mesh.shape["ctx"]
    split = Mesh(mesh.devices.reshape(dp, ctx // 2, 2), EVERY)
    ctx_axes = ("z", "core")
    tokens = P(ctx_axes, "dp", None)
    pair = P(ctx_axes, "dp")
    columns, units, unit_rows = P(None, EVERY), P(EVERY), P(EVERY, None)
    return jax.shard_map(
        local,
        mesh=split,
        in_specs=(
            tokens, P("dp", ctx_axes), P(), P(), pair, P(), P(), pair,
            P(), P(), P(), columns, units, unit_rows, P(), tokens,
        ),
        out_specs=(
            tokens, tokens, P(), P(), pair, P(), P(), pair,
            P(), P(), P(), columns, units, unit_rows, P(),
        ),
        check_vma=False,
    )
```

```python
import functools

import jax
import jax.numpy as jnp
from jax import lax
from jax.experimental import pallas as pl
from jax.experimental.pallas import tpu as pltpu
from jax.sharding import Mesh
from jax.sharding import PartitionSpec as P

HEADS = 17
HEAD_DIM = 64
EPSILON = 1e-05
MASKED = -1e30
SCALE = HEAD_DIM ** (-0.5)
GROUP = ("dp", "z")
EVERY = ("dp", "z", "core")
BF16 = jnp.bfloat16
F32 = jnp.float32
VMEM_BYTES = 48 * 1024 * 1024


def swapped(value):
    return lax.ppermute(value, "core", [(0, 1), (1, 0)])


def exchanged(value, axis, bit):
    return lax.ppermute(value, axis, [(i, i ^ bit) for i in range(lax.axis_size(axis))])


def axis_bits(axis):
    size = lax.axis_size(axis)
    return [(axis, 1 << b) for b in reversed(range(size.bit_length() - 1))]


def doubled(block, order):
    bits = axis_bits("dp") + axis_bits("z")
    held = block.reshape((1,) * len(bits) + block.shape)
    for place in order:
        held = jnp.concatenate([held, exchanged(held, *bits[place])], place)
    return held.reshape((-1,) + block.shape)


def halved(blocks, order):
    bits = axis_bits("dp") + axis_bits("z")
    block_shape = blocks.shape[1:]
    held = blocks.astype(BF16).reshape((2,) * len(bits) + block_shape)
    for place in order:
        keep = lax.slice_in_dim(held, 0, 1, axis=place)
        sent = exchanged(lax.slice_in_dim(held, 1, 2, axis=place), *bits[place])
        held = (keep.astype(F32) + sent.astype(F32)).astype(BF16)
    return held.reshape(block_shape)


def along_z(block):
    bits = axis_bits("z")
    held = block.reshape((1,) * len(bits) + block.shape)
    for place in range(len(bits)):
        held = jnp.concatenate([held, exchanged(held, *bits[place])], place)
    return held.reshape((-1,) + block.shape)


def summed_everywhere(value):
    for axis, bit in [("core", 1)] + axis_bits("z") + axis_bits("dp"):
        value = value + exchanged(value, axis, bit)
    return value


def reorder_kernel(take_ref, low_mine, high_mine, low_other, high_other, out_ref):
    rows, cut = out_ref.shape[1], low_mine.shape[1]
    mine = pl.program_id(0) % 2 == take_ref[take_ref.shape[0] - 1]

    def put(low_ref, high_ref):
        out_ref[0, :cut] = low_ref[0]
        out_ref[0, cut:] = high_ref[0, : rows - cut]

    @pl.when(mine)
    def _():
        put(low_mine, high_mine)

    @pl.when(jnp.logical_not(mine))
    def _():
        put(low_other, high_other)


def reorder_weights(take, low_mine, high_mine, low_other, high_other, rows):
    count, _, width = low_mine.shape

    def taken(array):
        return pl.BlockSpec((1,) + array.shape[1:], lambda i, t: (t[i // 2], 0, 0))

    parts = (low_mine, high_mine, low_other, high_other)
    return pl.pallas_call(
        reorder_kernel,
        grid_spec=pltpu.PrefetchScalarGridSpec(
            num_scalar_prefetch=1,
            grid=(2 * count,),
            in_specs=[taken(array) for array in parts],
            out_specs=pl.BlockSpec((1, rows, width), lambda i, t: (i, 0, 0)),
        ),
        out_shape=jax.ShapeDtypeStruct((2 * count, rows, width), BF16),
        compiler_params=pltpu.CompilerParams(vmem_limit_bytes=VMEM_BYTES),
        cost_estimate=pl.CostEstimate(flops=0, bytes_accessed=12 * count * rows * width, transcendentals=0),
        name="reorder_weights",
    )(take, *parts)


def copy_kernel(take_ref, in_ref, out_ref):
    out_ref[...] = in_ref[...]


def reorder_blocks(take, blocks):
    count, rows, width = blocks.shape
    return pl.pallas_call(
        copy_kernel,
        grid_spec=pltpu.PrefetchScalarGridSpec(
            num_scalar_prefetch=1,
            grid=(count,),
            in_specs=[pl.BlockSpec((1, rows, width), lambda i, t: (t[i], 0, 0))],
            out_specs=pl.BlockSpec((1, rows, width), lambda i, t: (i, 0, 0)),
        ),
        out_shape=jax.ShapeDtypeStruct(blocks.shape, BF16),
        compiler_params=pltpu.CompilerParams(vmem_limit_bytes=VMEM_BYTES),
        cost_estimate=pl.CostEstimate(flops=0, bytes_accessed=4 * count * rows * width, transcendentals=0),
        name="reorder_blocks",
    )(take, blocks)


def normalize(values, gain_row, shift_row):
    center = values - jnp.mean(values, -1, keepdims=True)
    spread = jnp.mean(center * center, -1, keepdims=True)
    return center * lax.rsqrt(spread + EPSILON) * gain_row + shift_row


def gelu_tanh(values):
    return jax.nn.gelu(values, approximate=True)


def contract(spec, left, right):
    return jnp.einsum(spec, left, right, preferred_element_type=F32)


def dot_over(left, right, left_dim, right_dim):
    return lax.dot_general(
        left, right, (((left_dim,), (right_dim,)), ((), ())), preferred_element_type=F32
    )


def scaled(block):
    return (block.astype(F32) * SCALE).astype(BF16)


def forward_kernel(z_ref, q_ref, k_ref, v_ref, row_ref, col_ref, out_ref, lse_ref, bias):
    keys, queries = bias.shape

    @pl.when(pl.program_id(0) == 0)
    def _():
        key_pos = lax.broadcasted_iota(jnp.int32, (keys, queries), 0)
        query_pos = z_ref[0] * queries + lax.broadcasted_iota(jnp.int32, (keys, queries), 1)
        docs = row_ref[z_ref[0]]
        same = col_ref[...].reshape(keys, 1) == docs
        bias[...] = jnp.where((key_pos <= query_pos) & same, 0.0, MASKED)

    scores = dot_over(k_ref[...], scaled(q_ref[...]), 0, 0) + bias[...]
    row_max = jnp.max(scores, 0, keepdims=True)
    powers = jnp.exp(scores - row_max)
    total = jnp.sum(powers, 0, keepdims=True)
    out = dot_over(v_ref[...], powers.astype(BF16), 1, 0) / total
    out_ref[...] = out.astype(BF16)
    lse_ref[0] = row_max + jnp.log(total)


def backward_kernel(
    z_ref, q_own, k_own, v_own, q_ref, k_ref, v_ref, do_ref, lse_ref, delta_ref,
    row_ref, col_ref, grad_ref, bias, dq, dk, dv,
):
    blocks, rows, _ = bias.shape
    z = z_ref[0]

    @pl.when(pl.program_id(0) == 0)
    def _():
        for j in range(blocks):

            @pl.when(j < z)
            def _():
                bias[j] = jnp.where(col_ref[j] == row_ref[z], 0.0, MASKED)

            @pl.when(j > z)
            def _():
                bias[j] = jnp.where(col_ref[z] == row_ref[j], 0.0, MASKED)

            @pl.when(j == z)
            def _():
                key_pos = lax.broadcasted_iota(jnp.int32, (rows, rows), 0)
                query_pos = lax.broadcasted_iota(jnp.int32, (rows, rows), 1)
                same = col_ref[z] == row_ref[z]
                bias[j] = jnp.where((key_pos <= query_pos) & same, 0.0, MASKED)

    query = scaled(q_own[...])
    key = k_own[...]
    value = v_own[...]
    d_out = do_ref[0]
    lse = lse_ref[0, 0]
    delta = delta_ref[0, 0]

    def pair(key_t, value_t, query_t, d_out_t, lse_row, delta_row, bias_block):
        scores = dot_over(key_t, query_t, 0, 0) + bias_block
        prob = jnp.exp(scores - lse_row)
        d_prob = dot_over(value_t, d_out_t, 0, 0)
        d_raw = (prob * (d_prob - delta_row)).astype(BF16)
        return prob.astype(BF16), d_raw

    prob, d_raw = pair(key, value, query, d_out, lse, delta, bias[z])
    dq[...] = dot_over(key, d_raw, 1, 0)
    dk[...] = dot_over(query, d_raw, 1, 1)
    dv[...] = dot_over(d_out, prob, 1, 1)

    for j in range(blocks):
        here = slice(j * rows, (j + 1) * rows)

        @pl.when(j < z)
        def _():
            key_j = k_ref[:, here]
            _, raw_j = pair(key_j, v_ref[:, here], query, d_out, lse, delta, bias[j])
            dq[...] += dot_over(key_j, raw_j, 1, 0)

        @pl.when(j > z)
        def _():
            query_j = scaled(q_ref[:, here])
            slot = jnp.bitwise_xor(z, j)
            d_out_j = do_ref[slot]
            prob_j, raw_j = pair(
                key, value, query_j, d_out_j, lse_ref[slot, 0], delta_ref[slot, 0], bias[j]
            )
            dk[...] += dot_over(query_j, raw_j, 1, 1)
            dv[...] += dot_over(d_out_j, prob_j, 1, 1)

    grad_ref[0] = (dq[...] * SCALE).astype(BF16)
    grad_ref[1] = dk[...].astype(BF16)
    grad_ref[2] = dv[...].astype(BF16)


def whole_block(array):
    return pl.BlockSpec(array.shape, lambda h, z: (0,) * array.ndim)


def head_specs(rows, length):
    own = [
        pl.BlockSpec((HEAD_DIM, rows), functools.partial(lambda p, h, z: (p * HEADS + h, z[0]), p))
        for p in range(3)
    ]
    full = [
        pl.BlockSpec((HEAD_DIM, length), functools.partial(lambda p, h, z: (p * HEADS + h, 0), p))
        for p in range(3)
    ]
    return own, full


def attend(z_index, joined_t, seg_rows, seg_cols, rows):
    length = joined_t.shape[1]
    own, full = head_specs(rows, length)
    return pl.pallas_call(
        forward_kernel,
        grid_spec=pltpu.PrefetchScalarGridSpec(
            num_scalar_prefetch=1,
            grid=(HEADS,),
            in_specs=[own[0], full[1], full[2], whole_block(seg_rows), whole_block(seg_cols)],
            out_specs=[
                pl.BlockSpec((HEAD_DIM, rows), lambda h, z: (h, 0)),
                pl.BlockSpec((1, 1, rows), lambda h, z: (h, 0, 0)),
            ],
            scratch_shapes=[pltpu.VMEM((length, rows), F32)],
        ),
        out_shape=[
            jax.ShapeDtypeStruct((HEADS * HEAD_DIM, rows), BF16),
            jax.ShapeDtypeStruct((HEADS, 1, rows), F32),
        ],
        compiler_params=pltpu.CompilerParams(vmem_limit_bytes=VMEM_BYTES),
        cost_estimate=pl.CostEstimate(
            flops=4 * HEADS * HEAD_DIM * rows * length,
            bytes_accessed=4 * HEADS * HEAD_DIM * length,
            transcendentals=HEADS * rows * length,
        ),
        name="attend",
    )(z_index, joined_t, joined_t, joined_t, seg_rows, seg_cols)


def attend_back(z_index, joined_t, d_att_all, lse_all, delta_all, seg_rows, seg_cols, rows):
    length = joined_t.shape[1]
    blocks = length // rows
    own, full = head_specs(rows, length)
    row_spec = pl.BlockSpec((blocks, 1, 1, rows), lambda h, z: (0, h, 0, 0))
    return pl.pallas_call(
        backward_kernel,
        grid_spec=pltpu.PrefetchScalarGridSpec(
            num_scalar_prefetch=1,
            grid=(HEADS,),
            in_specs=own
            + full
            + [
                pl.BlockSpec((blocks, HEAD_DIM, rows), lambda h, z: (0, h, 0)),
                row_spec,
                row_spec,
                whole_block(seg_rows),
                whole_block(seg_cols),
            ],
            out_specs=pl.BlockSpec((3, HEAD_DIM, rows), lambda h, z: (0, h, 0)),
            scratch_shapes=[pltpu.VMEM((blocks, rows, rows), F32)]
            + [pltpu.VMEM((HEAD_DIM, rows), F32)] * 3,
        ),
        out_shape=jax.ShapeDtypeStruct((3, HEADS * HEAD_DIM, rows), BF16),
        compiler_params=pltpu.CompilerParams(vmem_limit_bytes=VMEM_BYTES),
        cost_estimate=pl.CostEstimate(
            flops=8 * HEADS * HEAD_DIM * rows * length,
            bytes_accessed=8 * HEADS * HEAD_DIM * length,
            transcendentals=HEADS * rows * length,
        ),
        name="attend_back",
    )(z_index, *([joined_t] * 6), d_att_all, lse_all, delta_all, seg_rows, seg_cols)


def local(
    inputs,
    segments,
    ln1_gain,
    ln1_bias,
    qkv_weight,
    query_bias,
    value_bias,
    proj_weight,
    proj_bias,
    ln2_gain,
    ln2_bias,
    fc_weight,
    fc_bias,
    out_weight,
    out_bias,
    cotangent,
):
    part, seqs, width = inputs.shape
    dp, nz = lax.axis_size("dp"), lax.axis_size("z")
    z, core = lax.axis_index("z"), lax.axis_index("core")
    rows = 2 * part
    shard_rows, qkv_cols = qkv_weight.shape
    proj_cols = proj_weight.shape[1]
    units = fc_weight.shape[1]
    first = core == 0

    seg_row = jnp.pad(segments.reshape(1, seqs * part).astype(BF16), ((0, 7), (0, width - seqs * part)))
    packed = jnp.concatenate(
        [inputs[:, 0], inputs[:, 1], cotangent[:, 0], cotangent[:, 1], seg_row], 0
    )
    arrived = swapped(packed)
    low_part = jnp.where(first, packed, arrived)
    high_part = jnp.where(first, arrived, packed)

    def chip_rows(slot):
        here = slice(slot * part, (slot + 1) * part)
        return jnp.concatenate([low_part[here], high_part[here]], 0)

    def own_other(slot):
        zero, one = chip_rows(slot), chip_rows(slot + 1)
        return jnp.where(first, zero, one), jnp.where(first, one, zero)

    x_own, x_other = own_other(0)
    g_own, g_other = own_other(2)
    segs = [
        jnp.concatenate(
            [low_part[4 * part, i * part : (i + 1) * part], high_part[4 * part, i * part : (i + 1) * part]]
        )
        for i in range(2)
    ]
    seg_own = jnp.pad(jnp.where(first, segs[0], segs[1]).reshape(1, rows), ((0, 7), (0, width - rows)))

    bias_row = jnp.pad(fc_bias.reshape(1, units), ((0, 7), (0, qkv_cols + proj_cols - units)))
    pair_block = jnp.concatenate([jnp.concatenate([qkv_weight, proj_weight], 1), bias_row], 0)
    seq_all = lax.all_gather(jnp.concatenate([x_own, seg_own], 0), "z", axis=0, tiled=False)
    dp_places = list(range(dp.bit_length() - 1))
    z_places = [len(dp_places) + i for i in range(nz.bit_length() - 1)]
    grow = z_places + dp_places, z_places + dp_places[::-1]
    shrink = dp_places + z_places[::-1], dp_places[::-1] + z_places[::-1]
    take = (
        (jnp.arange(dp)[:, None] ^ lax.axis_index("dp")) * nz + (jnp.arange(nz)[None] ^ z)
    ).reshape(-1).astype(jnp.int32)
    cut = pair_block.shape[0] // 32 * 16
    low_half = doubled(pair_block[:cut], grow[0])
    high_half = doubled(pair_block[cut:], grow[1])
    out_block, low_half, high_half = lax.optimization_barrier((out_weight, low_half, high_half))
    w_out = doubled(out_block, grow[1]).reshape(-1, width)
    fc_block, seq_all = lax.optimization_barrier((fc_weight.T, seq_all))
    w_fc = lax.all_gather(fc_block, GROUP, axis=0, tiled=False)
    w_fc = reorder_blocks(take, w_fc)
    w_fc = w_fc.reshape(-1, width)
    b_fc = high_half[:, shard_rows - cut, :units].reshape(-1).astype(F32)
    w_pair = reorder_weights(
        jnp.concatenate([take, core.astype(jnp.int32).reshape(1)]),
        low_half,
        high_half,
        swapped(low_half),
        swapped(high_half),
        shard_rows,
    ).reshape(dp, width, qkv_cols + proj_cols)
    w_qkv, w_proj = w_pair[..., :qkv_cols], w_pair[..., qkv_cols:]

    x_all = seq_all[:, :rows].reshape(nz * rows, width)
    docs = seq_all[:, rows, :rows].astype(F32)
    seg_rows, seg_cols = docs.reshape(nz, 1, rows), docs.reshape(nz, rows, 1)
    z_index = z.astype(jnp.int32).reshape(1)

    h1_all = normalize(x_all.astype(F32), ln1_gain, ln1_bias).astype(BF16)
    qkv_bias = jnp.concatenate([query_bias, jnp.zeros_like(query_bias), value_bias])
    joined_t = (contract("cdn,rd->cnr", w_qkv, h1_all).reshape(3 * width, -1) + qkv_bias[:, None]).astype(BF16)
    att_t, lse = attend(z_index, joined_t, seg_rows, seg_cols, rows)
    lse_all = along_z(lse)
    att_other_t = swapped(att_t)

    x_f = x_own.astype(F32)
    branch = [contract("dr,dn->rn", att_t, w_proj[i]) for i in range(dp)]
    resid = x_f + jnp.concatenate(branch, 1) + proj_bias
    h2_f, ln2_back = jax.vjp(normalize, resid, ln2_gain, ln2_bias)
    h2 = h2_f.astype(BF16)
    h2_other = swapped(h2)

    def hidden(rows_in, gradient):
        pre = contract("rd,nd->rn", rows_in, w_fc) + b_fc
        act, gelu_back = jax.vjp(gelu_tanh, pre)
        d_pre = gelu_back(contract("rd,nd->rn", gradient, w_out))[0]
        return act.astype(BF16), d_pre.astype(BF16)

    act, d_pre = hidden(h2, g_own)
    act_other, d_pre_other = hidden(h2_other, g_other)
    d_h2_sent = swapped(contract("rn,nd->rd", d_pre_other, w_fc).astype(BF16))
    y_sent = swapped(contract("rn,nd->rd", act_other, w_out).astype(BF16))
    d_h2 = contract("rn,nd->rd", d_pre, w_fc) + d_h2_sent.astype(F32)
    output = (resid + contract("rn,nd->rd", act, w_out) + y_sent.astype(F32) + out_bias).astype(BF16)

    out_parts = contract("rn,rd->nd", act, g_own) + contract("rn,rd->nd", act_other, g_other)
    fc_parts = contract("rn,rd->nd", d_pre, h2) + contract("rn,rd->nd", d_pre_other, h2_other)
    out_grad = halved(out_parts.reshape(dp * nz, units, width), shrink[0])
    fc_grad = halved(fc_parts.reshape(dp * nz, units, width), shrink[1])
    d_resid_part, ln2_gain_grad, ln2_bias_grad = ln2_back(d_h2)
    d_resid = g_own.astype(F32) + d_resid_part
    d_branch = d_resid.astype(BF16)
    d_branch_other = swapped(d_branch)
    d_att_t = sum(
        contract("rn,dn->dr", d_branch[:, i * proj_cols : (i + 1) * proj_cols], w_proj[i])
        for i in range(dp)
    ).astype(BF16)
    products = d_att_t.astype(F32) * att_t.astype(F32)
    delta = jnp.sum(products.reshape(HEADS, HEAD_DIM, rows), 1, keepdims=True)
    d_att_all, delta_all = along_z(d_att_t), along_z(delta)

    fc_bias_part = jnp.sum(d_pre.astype(F32), 0) + jnp.sum(d_pre_other.astype(F32), 0)
    early_sum = summed_everywhere(
        jnp.stack([jnp.sum(g_own.astype(F32), 0), jnp.sum(d_branch.astype(F32), 0), ln2_gain_grad, ln2_bias_grad])
    )
    fc_bias_grad = fc_bias_part.reshape((dp, nz, units))
    for axis, dim in (("dp", 0), ("z", 1)):
        for _, bit in axis_bits(axis):
            keep = lax.slice_in_dim(fc_bias_grad, 0, bit, axis=dim)
            sent = lax.slice_in_dim(fc_bias_grad, bit, 2 * bit, axis=dim)
            fc_bias_grad = keep + exchanged(sent, axis, bit)
    fc_bias_grad = fc_bias_grad.reshape(units)

    grads_t = attend_back(z_index, joined_t, d_att_all, lse_all, delta_all, seg_rows, seg_cols, rows)
    dj_t = grads_t.reshape(3 * width, rows)
    dj_other_t = swapped(dj_t)

    def my_columns(block):
        split = block.reshape(block.shape[0], nz, 2, shard_rows)
        return jnp.where(first, split[:, :, 0], split[:, :, 1]).reshape(block.shape[0], -1)

    def my_rows(block_t):
        split = block_t.reshape(nz, 2, shard_rows, block_t.shape[1])
        return jnp.where(first, split[:, 0], split[:, 1]).reshape(-1, block_t.shape[1])

    h1_own = normalize(x_f, ln1_gain, ln1_bias).astype(BF16)
    h1_other = normalize(x_other.astype(F32), ln1_gain, ln1_bias).astype(BF16)
    h1_mine, h1_mine_other = my_columns(h1_own), my_columns(h1_other)
    att_mine, att_mine_other = my_rows(att_t), my_rows(att_other_t)
    qkv_parts, proj_parts = [], []
    for i in range(dp):
        span = slice(i * qkv_cols, (i + 1) * qkv_cols)
        qkv_part = contract("ra,nr->an", h1_mine, dj_t[span]) + contract(
            "ra,nr->an", h1_mine_other, dj_other_t[span]
        )
        span = slice(i * proj_cols, (i + 1) * proj_cols)
        proj_part = contract("ar,rn->an", att_mine, d_branch[:, span]) + contract(
            "ar,rn->an", att_mine_other, d_branch_other[:, span]
        )
        qkv_parts.append(qkv_part.astype(BF16))
        proj_parts.append(proj_part.astype(BF16))
    qkv_sent = reorder_blocks(take, jnp.concatenate(qkv_parts, 0).reshape(dp * nz, shard_rows, -1))
    proj_sent = reorder_blocks(take, jnp.concatenate(proj_parts, 0).reshape(dp * nz, shard_rows, -1))
    proj_grad = halved(proj_sent, shrink[0])
    qkv_grad = jnp.concatenate(
        [halved(qkv_sent[:, :cut], shrink[0]), halved(qkv_sent[:, cut:], shrink[1])], 0
    )

    _, ln1_back = jax.vjp(normalize, x_f, ln1_gain, ln1_bias)
    d_normed = sum(
        contract("nr,dn->rd", dj_t[i * qkv_cols : (i + 1) * qkv_cols], w_qkv[i]) for i in range(dp)
    )
    d_input_part, ln1_gain_grad, ln1_bias_grad = ln1_back(d_normed)
    input_grad = (d_resid + d_input_part).astype(BF16)
    dj_sums = jnp.sum(dj_t.astype(F32), 1)
    late_sum = summed_everywhere(
        jnp.stack([ln1_gain_grad, ln1_bias_grad, dj_sums[:width], dj_sums[2 * width :]])
    )

    def placed(block):
        mine = jnp.where(first, block[:part], block[part:])
        sent = swapped(jnp.where(first, block[part:], block[:part]))
        return jnp.stack([jnp.where(first, mine, sent), jnp.where(first, sent, mine)], 1)

    return (
        placed(output),
        placed(input_grad),
        late_sum[0],
        late_sum[1],
        qkv_grad.astype(F32),
        late_sum[2],
        late_sum[3],
        proj_grad.astype(F32),
        early_sum[1],
        early_sum[2],
        early_sum[3],
        fc_grad.astype(F32).T,
        fc_bias_grad,
        out_grad.astype(F32),
        early_sum[0],
    )


def solution(mesh):
    dp, ctx = mesh.shape["dp"], mesh.shape["ctx"]
    split = Mesh(mesh.devices.reshape(dp, ctx // 2, 2), EVERY)
    ctx_axes = ("z", "core")
    tokens = P(ctx_axes, "dp", None)
    pair = P(ctx_axes, "dp")
    columns, units, unit_rows = P(None, EVERY), P(EVERY), P(EVERY, None)
    return jax.shard_map(
        local,
        mesh=split,
        in_specs=(
            tokens, P("dp", ctx_axes), P(), P(), pair, P(), P(), pair,
            P(), P(), P(), columns, units, unit_rows, P(), tokens,
        ),
        out_specs=(
            tokens, tokens, P(), P(), pair, P(), P(), pair,
            P(), P(), P(), columns, units, unit_rows, P(),
        ),
        check_vma=False,
    )
```
